128 devices in a mesh: gz: 2 (over x_hi), row: 8 (over z, x_lo), col: 8 (over y, core).
Axes of the slice: x: 4 (x_hi: 2, x_lo: 2; x = x_hi * 2 + x_lo), y: 4, z: 4, core: 2. Of those that a mesh axis runs over, the one named last changes fastest.
Arguments:
- rhs_low: float32 [2, 8, 16, 256, 256], P('gz', 'col', 'row'), may hold values from -6 to 6
- rhs_top: float32 [3, 8, 16, 256, 256], P(None, 'col', 'row'), may hold values from -6 to 6
- inv_low: float32 [2, 8, 16, 256, 256], P('gz', 'col', 'row'), as said below
- inv_top: float32 [3, 8, 16, 256, 256], P(None, 'col', 'row'), as said below
- sizes_low: int32 [2, 8, 16], P('gz', 'col', 'row'), may hold values from 128 to 256, as said below
- sizes_top: int32 [3, 8, 16], P(None, 'col', 'row'), may hold values from 128 to 256, as said below
- blocks: float32 [2, 6, 8, 16, 8, 256, 256], P('gz', None, 'col', None, 'row'), may hold values from -0.078125 to 0.078125
- targets: int32 [2, 6, 8, 16, 8], P('gz', None, 'col', None, 'row'), may hold values from 0 to 127, as said below
Outputs:
- x_low: float32 [2, 8, 16, 256, 256], P('gz', 'col', 'row')
- x_top: float32 [3, 8, 16, 256, 256], P(None, 'col', 'row')
The draws below stay inside these ranges and needn't reach their ends.
Inputs may be any that keep to these rules, and one draw needn't show every extreme that they name: `inv_low`: each block is lower triangular. `inv_top`: each block is lower triangular. `sizes_low`: live column counts of the supernodes. `sizes_top`: live column counts of the supernodes. `targets`: an entry at list position e names a supernode t of the target level with (t // 2) % 8 == e.
All inputs are finite; a program needn't handle non-finite values.
Results may differ from the reference program's by a relative error of at most 0.0001.
Values sent between devices are 32-bit elements; how exact they have to be, the bound alone decides.
No kernel may reach another device: no remote copies, remote signals or barrier semaphores. Data moves between devices by JAX's collectives and lax.ppermute only.
A program may use at most 128 MiB of HBM per device.

```python
import math
import jax
import jax.numpy as jnp
from jax import lax

W = 256
R = 256
SUP_DEV = 2
K = 1
PAIRS = 6
SUBTREES = 2
GRID_ROWS = 8
GRID_COLS = 8
COL_SUPS = 16


def lower_factor(key, shape):
    block_width = shape[-1]
    key_off, key_diag = jax.random.split(key)
    spread = jax.random.normal(key_off, shape, jnp.float32)
    diagonal_block = jax.random.uniform(key_diag, shape[:-1] + (1,), jnp.float32, 0.5, 1.5)
    row_ids = lax.broadcasted_iota(jnp.int32, (block_width, block_width), 0)
    col_ids = lax.broadcasted_iota(jnp.int32, (block_width, block_width), 1)
    strict = (row_ids > col_ids).astype(jnp.float32)
    identity_mask = (row_ids == col_ids).astype(jnp.float32)
    return spread * strict / math.sqrt(block_width) + diagonal_block * identity_mask


def draw_inv_low(key, part):
    shape = (SUBTREES, GRID_COLS, COL_SUPS, W, W)
    return lower_factor(key, shape)


def draw_inv_top(key, part):
    shape = (3, GRID_COLS, COL_SUPS, W, W)
    return lower_factor(key, shape)


def live_counts(key, shape):
    values = jax.random.randint(key, shape, W // 2, W + 1, dtype=jnp.int32)
    values = values.at[..., 0, 0].set(W)
    return values.at[..., -1, -1].set(W // 2)


def draw_sizes_low(key, part):
    return live_counts(key, (SUBTREES, GRID_COLS, COL_SUPS))


def draw_sizes_top(key, part):
    return live_counts(key, (3, GRID_COLS, COL_SUPS))


def draw_targets(key, part):
    leading = SUBTREES * PAIRS * GRID_COLS * COL_SUPS * GRID_ROWS
    choice_count = GRID_COLS * SUP_DEV
    scores = jax.random.randint(key, (leading, choice_count), 0, 1 << 20, dtype=jnp.int32) * choice_count + jnp.arange(choice_count, dtype=jnp.int32)[None, :]
    picked = jnp.argsort(scores, axis=1)[:, :K].astype(jnp.int32)
    column_pick = picked // SUP_DEV
    within_pick = picked % SUP_DEV
    group_of_rows = (jnp.arange(leading, dtype=jnp.int32) % GRID_ROWS)[:, None]
    chosen = column_pick * COL_SUPS + group_of_rows * SUP_DEV + within_pick
    return chosen.reshape(SUBTREES, PAIRS, GRID_COLS, COL_SUPS, GRID_ROWS * K).astype(jnp.int32)


def level_of(stream_key, dims, cuts, least, largest):
    def one(dim, shards_of):
        draws = jax.random.uniform(jax.random.fold_in(jax.random.fold_in(stream_key, 6), dim), (shards_of,), jnp.float32, least / len(cuts), largest / len(cuts))
        return jnp.repeat(jnp.exp(draws), dims[dim] // shards_of).reshape((-1,) + (1,) * (len(dims) - dim - 1))

    factor_of = one(*cuts[0])
    for cut in cuts[1:]:
        factor_of = factor_of * one(*cut)
    return factor_of


def bell_draw(rng, shape, scale, most, shards=(), held_as=jnp.bfloat16):
    result = jax.random.normal(rng, shape, jnp.float32) * scale
    if len(shards) > 0:
        result = level_of(rng, shape, shards, -0.22, 0.18) * result
    return jnp.clip(result, min=-most, max=most).astype(held_as)


def setup_inputs(seed: int = 0) -> dict:
    seeds = jax.random.split(jax.random.key(seed), 9)
    return {
        "rhs_low": bell_draw(seeds[0], (SUBTREES, GRID_COLS, COL_SUPS, W, R), 1.0, 6.0, ((0, 2), (1, 8), (2, 8)), jnp.float32),
        "rhs_top": bell_draw(seeds[1], (3, GRID_COLS, COL_SUPS, W, R), 1.0, 6.0, ((1, 8), (2, 8)), jnp.float32),
        "inv_low": draw_inv_low(jax.random.fold_in(seeds[8], 71), 0),
        "inv_top": draw_inv_top(jax.random.fold_in(seeds[8], 71), 0),
        "sizes_low": draw_sizes_low(jax.random.fold_in(seeds[8], 71), 0),
        "sizes_top": draw_sizes_top(jax.random.fold_in(seeds[8], 71), 0),
        "blocks": bell_draw(seeds[6], (SUBTREES, PAIRS, GRID_COLS, COL_SUPS, GRID_ROWS * K, W, W), (W * 24) ** -0.5, 0.078125, ((0, 2), (2, 8), (4, 8)), jnp.float32),
        "targets": draw_targets(jax.random.fold_in(seeds[8], 71), 0),
    }


def solve_level(right_hand_side, inverse_factor, live_count, update_block):
    row_ids = jnp.arange(W, dtype=jnp.int32)[:, None]
    live_rows = (row_ids < live_count[..., None, None]).astype(jnp.float32)
    solved = jnp.einsum('...ab,...br->...ar', inverse_factor, right_hand_side - update_block, precision=lax.Precision.HIGHEST)
    return solved * live_rows


def contribute(blocks, targets, pair_index, solution):
    total = jnp.zeros((GRID_COLS * COL_SUPS, W, R), jnp.float32)
    for subtree in range(SUBTREES):
        source = solution[subtree] if solution.ndim == 5 else solution
        product = jnp.einsum('cseab,csbr->csear', blocks[subtree, pair_index], source, precision=lax.Precision.HIGHEST)
        total = total + jax.ops.segment_sum(product.reshape(-1, W, R), targets[subtree, pair_index].reshape(-1), num_segments=GRID_COLS * COL_SUPS)
    return total.reshape(GRID_COLS, COL_SUPS, W, R)


def reference(rhs_low, rhs_top, inv_low, inv_top, sizes_low, sizes_top, blocks, targets):
    level_zero = solve_level(rhs_low, inv_low, sizes_low, jnp.zeros_like(rhs_low))
    update_one = contribute(blocks, targets, 0, level_zero)
    first_level = solve_level(rhs_top[0], inv_top[0], sizes_top[0], update_one)
    update_two = contribute(blocks, targets, 1, level_zero) + contribute(blocks, targets, 3, first_level)
    level_two = solve_level(rhs_top[1], inv_top[1], sizes_top[1], update_two)
    update_three = contribute(blocks, targets, 2, level_zero) + contribute(blocks, targets, 4, first_level) + contribute(blocks, targets, 5, level_two)
    level_three = solve_level(rhs_top[2], inv_top[2], sizes_top[2], update_three)
    return level_zero, jnp.stack([first_level, level_two, level_three])
```

```python
import functools

import jax
import jax.numpy as jnp
from jax import lax
from jax.experimental import pallas as pl
from jax.experimental.pallas import tpu as pltpu
from jax.sharding import Mesh, PartitionSpec as P

CHUNKS = 2
X_LO = 2
CORES = 2


def split(value):
    high = value.astype(jnp.bfloat16)
    low = (value - high.astype(jnp.float32)).astype(jnp.bfloat16)
    return high, low


def product(left, right):
    left_high, left_low = split(left)
    right_high, right_low = split(right)
    columns = right.shape[1]
    both = jnp.dot(
        left_high,
        jnp.concatenate([right_high, right_low], axis=1),
        preferred_element_type=jnp.float32,
    )
    cross = jnp.dot(left_low, right_high, preferred_element_type=jnp.float32)
    return both[:, :columns] + (both[:, columns:] + cross)


def contribute_kernel(pair, places, seeded, order_ref, slots_ref, blocks_ref, *refs):
    count = len(set(array for array, _ in places))
    shared_refs = refs[:count]
    refs = refs[count:]
    if seeded:
        seed_kept, seed_sent, kept_ref, sent_ref = refs
    else:
        kept_ref, sent_ref = refs
    step = pl.program_id(0)
    half = kept_ref.shape[0]
    per_row = blocks_ref.shape[1]

    @pl.when(step == 0)
    def _():
        if seeded:
            kept_ref[...] = seed_kept[...]
            sent_ref[...] = seed_sent[...]
        else:
            kept_ref[...] = jnp.zeros_like(kept_ref)
            sent_ref[...] = jnp.zeros_like(sent_ref)

    row = order_ref[step]

    def add(array, offset):
        for member in range(per_row):
            value = product(blocks_ref[0, member], shared_refs[array][offset + member])
            slot = slots_ref[pair, row * per_row + member]

            @pl.when(slot < half)
            def _():
                kept_ref[slot] += value

            @pl.when(slot >= half)
            def _():
                sent_ref[slot - half] += value

    for index, (array, offset) in enumerate(places):
        pl.when(step == index)(functools.partial(add, array, offset))


def contribute(pair, blocks, slots, order, arrays, places, seed):
    per_row = blocks.shape[1] // len(places)
    rows = blocks.shape[2]
    columns = arrays[0].shape[-1]
    half = blocks.shape[1] // 2
    whole = lambda shape: pl.BlockSpec(shape, lambda step, order, slots: (0,) * len(shape))
    out = jax.ShapeDtypeStruct((half, rows, columns), jnp.float32)
    seeds = [] if seed is None else list(seed)
    return pl.pallas_call(
        functools.partial(contribute_kernel, pair, places, seed is not None),
        grid_spec=pltpu.PrefetchScalarGridSpec(
            num_scalar_prefetch=2,
            grid=(len(places),),
            in_specs=[
                pl.BlockSpec(
                    (1, per_row, rows, rows),
                    lambda step, order, slots: (pair, order[step], 0, 0),
                )
            ]
            + [whole(array.shape) for array in arrays]
            + [whole(out.shape) for _ in seeds],
            out_specs=[whole(out.shape), whole(out.shape)],
        ),
        out_shape=[out, out],
        compiler_params=pltpu.CompilerParams(vmem_limit_bytes=32 * 1024 * 1024),
        cost_estimate=pl.CostEstimate(
            flops=6 * blocks.shape[1] * rows * rows * columns,
            bytes_accessed=4 * blocks.shape[1] * (rows * rows + 3 * rows * columns),
            transcendentals=0,
        ),
    )(order, slots, blocks, *arrays, *seeds)


def ring(value, axis, shift):
    size = lax.axis_size(axis)
    return lax.ppermute(value, axis, [(i, (i + shift) % size) for i in range(size)])


def solve(inverse, right_hand_side, live_count):
    solved = jnp.einsum(
        "itc,icq->itq", inverse, right_hand_side, precision=lax.Precision.HIGH
    )
    row_ids = lax.broadcasted_iota(jnp.int32, (1, inverse.shape[1], 1), 1)
    return jnp.where(row_ids < live_count[:, None, None], solved, 0.0)


def row_order(places):
    z = lax.axis_index("z")
    lo = lax.axis_index("xl")
    size = lax.axis_size("z")
    rows = [((z - shift) % size) * X_LO + (lo ^ other) for shift, other in places]
    return jnp.stack(rows).astype(jnp.int32)


def along_z(value):
    return [ring(value, "z", shift) for shift in range(1, lax.axis_size("z"))]


def gather_x_first(own):
    per_row = own.shape[0]
    other = ring(own, "xl", 1)
    pair = jnp.concatenate([own, other])
    arrays = [own, other] + along_z(pair)
    spots = [(0, 0), (1, 0)]
    where = [(0, 0), (0, 1)]
    for shift in range(1, lax.axis_size("z")):
        for member in range(X_LO):
            spots.append((1 + shift, member * per_row))
            where.append((shift, member))
    return arrays, spots, row_order(where)


def gather_z_first(own):
    per_row = own.shape[0]
    others = along_z(own)
    arrays = [own] + others
    across = ring(jnp.concatenate(arrays), "xl", 1)
    count = len(arrays)
    spots = [(k, 0) for k in range(count)] + [(count, k * per_row) for k in range(count)]
    where = [(k, 0) for k in range(count)] + [(k, 1) for k in range(count)]
    return arrays + [across], spots, row_order(where)


def gather_shared(own):
    per_row = own.shape[0]
    arrays = [own] + along_z(own)
    count = len(arrays)
    near = jnp.concatenate(arrays[: count // 2])
    far = jnp.concatenate(arrays[count // 2 :])
    x_size = lax.axis_size("gz") * X_LO
    axes = ("gz", "xl")
    up = lax.ppermute(near, axes, [(i, (i + 1) % x_size) for i in range(x_size)])
    down = lax.ppermute(far, axes, [(i, (i - 1) % x_size) for i in range(x_size)])
    spots = [(k, 0) for k in range(count)]
    spots += [(count + k // (count // 2), (k % (count // 2)) * per_row) for k in range(count)]
    where = [(k, 0) for k in range(count)] + [(k, 1) for k in range(count)]
    return arrays + [up, down], spots, row_order(where)


def reduce_update(kept, sent):
    total = kept + ring(sent, "core", 1)
    size = lax.axis_size("y")
    per_device = total.shape[0] // size
    parts = total.reshape((size, per_device) + total.shape[1:])
    mine = parts[0]
    for shift in range(1, size):
        mine = mine + ring(parts[shift], "y", shift)
    return mine + ring(mine, "gz", 1)


def on_device(rhs_low, rhs_top, inv_low, inv_top, sizes_low, sizes_top, blocks, targets):
    rhs_low, inv_low, sizes_low = rhs_low[0, 0], inv_low[0, 0], sizes_low[0, 0]
    rhs_top, inv_top, sizes_top = rhs_top[:, 0], inv_top[:, 0], sizes_top[:, 0]
    blocks = blocks[0, :, 0, :, 0]
    targets = targets[0, :, 0, :, 0]
    per_device = sizes_low.shape[0]
    col_sups = blocks.shape[1]
    y_size = lax.axis_size("y")
    group = targets // col_sups
    turned = (group // CORES - lax.axis_index("y")) % y_size
    swapped = (group % CORES + lax.axis_index("core")) % CORES
    slots = (swapped * y_size + turned) * per_device + targets % per_device
    slots = slots.astype(jnp.int32)

    width = rhs_low.shape[-1] // CHUNKS
    low_parts = []
    top_parts = []
    for chunk in range(CHUNKS):
        cut = slice(chunk * width, (chunk + 1) * width)
        apply = functools.partial(contribute, blocks=blocks, slots=slots)
        low = solve(inv_low, rhs_low[:, :, cut], sizes_low)
        arrays, spots, order = (gather_x_first if chunk % 2 == 0 else gather_z_first)(low)
        use = lambda pair, seed: contribute(pair, blocks, slots, order, arrays, spots, seed)
        first = reduce_update(*use(0, None))
        second_seed = use(1, None)
        third_seed = use(2, None)
        level_one = solve(inv_top[0], rhs_top[0][:, :, cut] - first, sizes_top[0])
        arrays, spots, order = gather_shared(level_one)
        second = reduce_update(*use(3, second_seed))
        third_seed = use(4, third_seed)
        level_two = solve(inv_top[1], rhs_top[1][:, :, cut] - second, sizes_top[1])
        arrays, spots, order = gather_shared(level_two)
        third = reduce_update(*use(5, third_seed))
        level_three = solve(inv_top[2], rhs_top[2][:, :, cut] - third, sizes_top[2])
        low_parts.append(low)
        top_parts.append(jnp.stack([level_one, level_two, level_three]))
    x_low = jnp.concatenate(low_parts, axis=-1)
    x_top = jnp.concatenate(top_parts, axis=-1)
    return x_low[None, None], x_top[:, None]


def solution(mesh):
    subtrees, rows, columns = (mesh.shape[name] for name in ("gz", "row", "col"))
    sizes = (subtrees, rows // X_LO, X_LO, columns // CORES, CORES)
    fine = Mesh(mesh.devices.reshape(sizes), ("gz", "z", "xl", "y", "core"))
    row, col = ("z", "xl"), ("y", "core")
    placed = (
        P("gz", col, row, None, None),
        P(None, col, row, None, None),
        P("gz", col, row, None, None),
        P(None, col, row, None, None),
        P("gz", col, row),
        P(None, col, row),
        P("gz", None, col, None, row, None, None),
        P("gz", None, col, None, row),
    )
    return jax.shard_map(
        on_device,
        mesh=fine,
        in_specs=placed,
        out_specs=(P("gz", col, row, None, None), P(None, col, row, None, None)),
        check_vma=False,
    )
```

```python
import functools

import jax
import jax.numpy as jnp
from jax import lax
from jax.experimental import pallas as pl
from jax.experimental.pallas import tpu as pltpu
from jax.sharding import Mesh, PartitionSpec as P

CHUNKS = 2
X_LO = 2
CORES = 2


def split(value):
    high = value.astype(jnp.bfloat16)
    low = (value - high.astype(jnp.float32)).astype(jnp.bfloat16)
    return high, low


def product(left, right):
    left_high, left_low = split(left)
    right_high, right_low = split(right)
    columns = right.shape[1]
    both = jnp.dot(
        left_high,
        jnp.concatenate([right_high, right_low], axis=1),
        preferred_element_type=jnp.float32,
    )
    cross = jnp.dot(left_low, right_high, preferred_element_type=jnp.float32)
    return both[:, :columns] + (both[:, columns:] + cross)


def contribute_kernel(pair, places, seeded, order_ref, slots_ref, blocks_ref, *refs):
    shared_refs = refs[: len(refs) - 1 - seeded]
    total_ref = refs[-1]
    per_row = blocks_ref.shape[0] // len(places)
    if seeded:
        total_ref[...] = refs[-2][...]
    else:
        total_ref[...] = jnp.zeros_like(total_ref)
    for index, (array, offset) in enumerate(places):
        for member in range(per_row):
            name = order_ref[index] * per_row + member
            value = product(blocks_ref[name], shared_refs[array][offset + member])
            total_ref[slots_ref[pair, name]] += value


def stage_kernel(pair, blocks_ref, staged_ref, done):
    pieces = done.shape[0]
    count = staged_ref.shape[0] // pieces
    copies = []
    for piece in range(pieces):
        part = pl.ds(piece * count, count)
        copies.append(
            pltpu.make_async_copy(
                blocks_ref.at[pair, part], staged_ref.at[part], done.at[piece]
            )
        )
    for copy in copies:
        copy.start()
    for copy in copies:
        copy.wait()


def stage(pair, blocks):
    return pl.pallas_call(
        functools.partial(stage_kernel, pair),
        in_specs=[pl.BlockSpec(memory_space=pl.ANY)],
        out_specs=pl.BlockSpec(memory_space=pltpu.VMEM),
        out_shape=jax.ShapeDtypeStruct(blocks.shape[1:], blocks.dtype),
        scratch_shapes=[pltpu.SemaphoreType.DMA((4,))],
        compiler_params=pltpu.CompilerParams(vmem_limit_bytes=32 * 1024 * 1024),
        cost_estimate=pl.CostEstimate(
            flops=0, bytes_accessed=8 * blocks[0].size, transcendentals=0
        ),
    )(blocks)


def contribute(pair, blocks, slots, order, arrays, places, seed):
    count, rows = blocks.shape[0], blocks.shape[1]
    columns = arrays[0].shape[-1]
    scalars = pl.BlockSpec(memory_space=pltpu.SMEM)
    local = pl.BlockSpec(memory_space=pltpu.VMEM)
    seeds = [] if seed is None else [seed]
    return pl.pallas_call(
        functools.partial(contribute_kernel, pair, places, len(seeds)),
        in_specs=[scalars, scalars] + [local] * (1 + len(arrays) + len(seeds)),
        out_specs=local,
        out_shape=jax.ShapeDtypeStruct((count, rows, columns), jnp.float32),
        compiler_params=pltpu.CompilerParams(vmem_limit_bytes=32 * 1024 * 1024),
        cost_estimate=pl.CostEstimate(
            flops=60 * count * rows * rows * columns,
            bytes_accessed=40 * count * (rows * rows + 3 * rows * columns),
            transcendentals=0,
        ),
    )(order, slots, blocks, *arrays, *seeds)


def ring(value, axis, shift):
    size = lax.axis_size(axis)
    return lax.ppermute(value, axis, [(i, (i + shift) % size) for i in range(size)])


def solve(inverse, right_hand_side, live_count):
    solved = jnp.einsum(
        "itc,icq->itq", inverse, right_hand_side, precision=lax.Precision.HIGH
    )
    row_ids = lax.broadcasted_iota(jnp.int32, (1, inverse.shape[1], 1), 1)
    return jnp.where(row_ids < live_count[:, None, None], solved, 0.0)


def row_order(places):
    z = lax.axis_index("z")
    lo = lax.axis_index("xl")
    size = lax.axis_size("z")
    rows = [((z - shift) % size) * X_LO + (lo ^ other) for shift, other in places]
    return jnp.stack(rows).astype(jnp.int32)


def along_z(value):
    return [ring(value, "z", shift) for shift in range(1, lax.axis_size("z"))]


def gather_low(first, last):
    per_row = first.shape[0]
    others = along_z(last)
    near = ring(first, "xl", 1)
    pair, others = lax.optimization_barrier((jnp.concatenate([first, near]), others))
    arrays = [last] + others
    count = len(arrays)
    across = ring(jnp.concatenate(arrays), "xl", 1)
    last_spots = [(k, 0) for k in range(count)] + [(count, k * per_row) for k in range(count)]
    last_where = [(k, 0) for k in range(count)] + [(k, 1) for k in range(count)]
    spots = [(0, 0), (1, 0)]
    where = [(0, 0), (0, 1)]
    for shift in range(1, count):
        for member in range(X_LO):
            spots.append((1 + shift, member * per_row))
            where.append((shift, member))
    return (
        ([first, near] + along_z(pair), spots, row_order(where)),
        (arrays + [across], last_spots, row_order(last_where)),
    )


def gather_shared(own):
    per_row = own.shape[0]
    arrays = [own] + along_z(own)
    count = len(arrays)
    near = jnp.concatenate(arrays[: count // 2])
    far = jnp.concatenate(arrays[count // 2 :])
    x_size = lax.axis_size("gz") * X_LO
    axes = ("gz", "xl")
    up = lax.ppermute(near, axes, [(i, (i + 1) % x_size) for i in range(x_size)])
    down = lax.ppermute(far, axes, [(i, (i - 1) % x_size) for i in range(x_size)])
    spots = [(k, 0) for k in range(count)]
    spots += [(count + k // (count // 2), (k % (count // 2)) * per_row) for k in range(count)]
    where = [(k, 0) for k in range(count)] + [(k, 1) for k in range(count)]
    return arrays + [up, down], spots, row_order(where)


def reduce_update(sums):
    half = sums.shape[0] // 2
    total = sums[:half] + ring(sums[half:], "core", 1)
    size = lax.axis_size("y")
    per_device = total.shape[0] // size
    parts = total.reshape((size, per_device) + total.shape[1:])
    mine = parts[0]
    for shift in range(1, size):
        mine = mine + ring(parts[shift], "y", shift)
    return mine + ring(mine, "gz", 1)


def on_device(rhs_low, rhs_top, inv_low, inv_top, sizes_low, sizes_top, blocks, targets):
    rhs_low, inv_low, sizes_low = rhs_low[0, 0], inv_low[0, 0], sizes_low[0, 0]
    rhs_top, inv_top, sizes_top = rhs_top[:, 0], inv_top[:, 0], sizes_top[:, 0]
    blocks = blocks[0, :, 0, :, 0]
    targets = targets[0, :, 0, :, 0]
    per_device = sizes_low.shape[0]
    col_sups = blocks.shape[1]
    y_size = lax.axis_size("y")
    group = targets // col_sups
    turned = (group // CORES - lax.axis_index("y")) % y_size
    swapped = (group % CORES + lax.axis_index("core")) % CORES
    slots = (swapped * y_size + turned) * per_device + targets % per_device
    slots = slots.astype(jnp.int32)

    width = rhs_low.shape[-1] // CHUNKS
    top_parts = []
    pair_blocks = [stage(pair, blocks) for pair in range(blocks.shape[0])]
    cuts = [slice(chunk * width, (chunk + 1) * width) for chunk in range(CHUNKS)]
    lows = [solve(inv_low, rhs_low[:, :, cut], sizes_low) for cut in cuts]
    gathered = gather_low(*lows)
    for chunk, cut in enumerate(cuts):
        arrays, spots, order = gathered[chunk]
        use = lambda pair, seed: contribute(
            pair, pair_blocks[pair], slots, order, arrays, spots, seed
        )
        first = reduce_update(use(0, None))
        second_seed = use(1, None)
        third_seed = use(2, None)
        level_one = solve(inv_top[0], rhs_top[0][:, :, cut] - first, sizes_top[0])
        arrays, spots, order = gather_shared(level_one)
        second = reduce_update(use(3, second_seed))
        third_seed = use(4, third_seed)
        level_two = solve(inv_top[1], rhs_top[1][:, :, cut] - second, sizes_top[1])
        arrays, spots, order = gather_shared(level_two)
        third = reduce_update(use(5, third_seed))
        level_three = solve(inv_top[2], rhs_top[2][:, :, cut] - third, sizes_top[2])
        top_parts.append(jnp.stack([level_one, level_two, level_three]))
    x_low = jnp.concatenate(lows, axis=-1)
    x_top = jnp.concatenate(top_parts, axis=-1)
    return x_low[None, None], x_top[:, None]


def solution(mesh):
    subtrees, rows, columns = (mesh.shape[name] for name in ("gz", "row", "col"))
    sizes = (subtrees, rows // X_LO, X_LO, columns // CORES, CORES)
    fine = Mesh(mesh.devices.reshape(sizes), ("gz", "z", "xl", "y", "core"))
    row, col = ("z", "xl"), ("y", "core")
    placed = (
        P("gz", col, row, None, None),
        P(None, col, row, None, None),
        P("gz", col, row, None, None),
        P(None, col, row, None, None),
        P("gz", col, row),
        P(None, col, row),
        P("gz", None, col, None, row, None, None),
        P("gz", None, col, None, row),
    )
    return jax.shard_map(
        on_device,
        mesh=fine,
        in_specs=placed,
        out_specs=(P("gz", col, row, None, None), P(None, col, row, None, None)),
        check_vma=False,
    )
```

```python
import functools

import jax
import jax.numpy as jnp
from jax import lax
from jax.experimental import pallas as pl
from jax.experimental.pallas import tpu as pltpu
from jax.sharding import Mesh, PartitionSpec as P

CHUNKS = 2
X_LO = 2
CORES = 2


def split(value):
    high = value.astype(jnp.bfloat16)
    low = (value - high.astype(jnp.float32)).astype(jnp.bfloat16)
    return high, low


def product(left, right):
    left_high, left_low = split(left)
    right_high, right_low = split(right)
    columns = right.shape[1]
    both = jnp.dot(
        left_high,
        jnp.concatenate([right_high, right_low], axis=1),
        preferred_element_type=jnp.float32,
    )
    cross = jnp.dot(left_low, right_high, preferred_element_type=jnp.float32)
    return both[:, :columns] + (both[:, columns:] + cross)


def contribute_kernel(pair, places, seeded, order_ref, slots_ref, blocks_ref, *refs):
    shared_refs = refs[: len(refs) - 1 - seeded]
    total_ref = refs[-1]
    per_row = blocks_ref.shape[0] // len(places)
    if seeded:
        total_ref[...] = refs[-2][...]
    else:
        total_ref[...] = jnp.zeros_like(total_ref)
    for index, (array, offset) in enumerate(places):
        for member in range(per_row):
            name = order_ref[index] * per_row + member
            value = product(blocks_ref[name], shared_refs[array][offset + member])
            total_ref[slots_ref[pair, name]] += value


def stage_kernel(pair, blocks_ref, staged_ref, done):
    pieces = done.shape[0]
    count = staged_ref.shape[0] // pieces
    copies = []
    for piece in range(pieces):
        part = pl.ds(piece * count, count)
        copies.append(
            pltpu.make_async_copy(
                blocks_ref.at[pair, part], staged_ref.at[part], done.at[piece]
            )
        )
    for copy in copies:
        copy.start()
    for copy in copies:
        copy.wait()


def stage(pair, blocks):
    return pl.pallas_call(
        functools.partial(stage_kernel, pair),
        in_specs=[pl.BlockSpec(memory_space=pl.ANY)],
        out_specs=pl.BlockSpec(memory_space=pltpu.VMEM),
        out_shape=jax.ShapeDtypeStruct(blocks.shape[1:], blocks.dtype),
        scratch_shapes=[pltpu.SemaphoreType.DMA((4,))],
        compiler_params=pltpu.CompilerParams(vmem_limit_bytes=32 * 1024 * 1024),
        cost_estimate=pl.CostEstimate(
            flops=0, bytes_accessed=8 * blocks[0].size, transcendentals=0
        ),
    )(blocks)


def contribute(pair, blocks, slots, order, arrays, places, seed):
    count, rows = blocks.shape[0], blocks.shape[1]
    columns = arrays[0].shape[-1]
    scalars = pl.BlockSpec(memory_space=pltpu.SMEM)
    local = pl.BlockSpec(memory_space=pltpu.VMEM)
    seeds = [] if seed is None else [seed]
    return pl.pallas_call(
        functools.partial(contribute_kernel, pair, places, len(seeds)),
        in_specs=[scalars, scalars] + [local] * (1 + len(arrays) + len(seeds)),
        out_specs=local,
        out_shape=jax.ShapeDtypeStruct((count, rows, columns), jnp.float32),
        compiler_params=pltpu.CompilerParams(vmem_limit_bytes=32 * 1024 * 1024),
        cost_estimate=pl.CostEstimate(
            flops=60 * count * rows * rows * columns,
            bytes_accessed=40 * count * (rows * rows + 3 * rows * columns),
            transcendentals=0,
        ),
    )(order, slots, blocks, *arrays, *seeds)


def ring(value, axis, shift):
    size = lax.axis_size(axis)
    return lax.ppermute(value, axis, [(i, (i + shift) % size) for i in range(size)])


def solve(inverse, right_hand_side, live_count):
    solved = jnp.einsum(
        "itc,icq->itq", inverse, right_hand_side, precision=lax.Precision.HIGH
    )
    row_ids = lax.broadcasted_iota(jnp.int32, (1, inverse.shape[1], 1), 1)
    return jnp.where(row_ids < live_count[:, None, None], solved, 0.0)


def row_order(places):
    z = lax.axis_index("z")
    lo = lax.axis_index("xl")
    size = lax.axis_size("z")
    rows = [((z - shift) % size) * X_LO + (lo ^ other) for shift, other in places]
    return jnp.stack(rows).astype(jnp.int32)


def along_z(value):
    return [ring(value, "z", shift) for shift in range(1, lax.axis_size("z"))]


def gather_low(first, last):
    per_row = first.shape[0]
    others = along_z(last)
    near = ring(first, "xl", 1)
    pair, others = lax.optimization_barrier((jnp.concatenate([first, near]), others))
    arrays = [last] + others
    count = len(arrays)
    across = ring(jnp.concatenate(arrays), "xl", 1)
    last_spots = [(k, 0) for k in range(count)] + [(count, k * per_row) for k in range(count)]
    last_where = [(k, 0) for k in range(count)] + [(k, 1) for k in range(count)]
    spots = [(0, 0), (1, 0)]
    where = [(0, 0), (0, 1)]
    for shift in range(1, count):
        for member in range(X_LO):
            spots.append((1 + shift, member * per_row))
            where.append((shift, member))
    return (
        ([first, near] + along_z(pair), spots, row_order(where)),
        (arrays + [across], last_spots, row_order(last_where)),
    )


def gather_shared(own):
    per_row = own.shape[0]
    arrays = [own] + along_z(own)
    count = len(arrays)
    near = jnp.concatenate(arrays[: count // 2])
    far = jnp.concatenate(arrays[count // 2 :])
    x_size = lax.axis_size("gz") * X_LO
    axes = ("gz", "xl")
    up = lax.ppermute(near, axes, [(i, (i + 1) % x_size) for i in range(x_size)])
    down = lax.ppermute(far, axes, [(i, (i - 1) % x_size) for i in range(x_size)])
    spots = [(k, 0) for k in range(count)]
    spots += [(count + k // (count // 2), (k % (count // 2)) * per_row) for k in range(count)]
    where = [(k, 0) for k in range(count)] + [(k, 1) for k in range(count)]
    return arrays + [up, down], spots, row_order(where)


def reduce_update(sums):
    half = sums.shape[0] // 2
    total = sums[:half] + ring(sums[half:], "core", 1)
    size = lax.axis_size("y")
    per_device = total.shape[0] // size
    parts = total.reshape((size, per_device) + total.shape[1:])
    mine = parts[0]
    for shift in range(1, size):
        mine = mine + ring(parts[shift], "y", shift)
    return mine + ring(mine, "gz", 1), total


def on_device(rhs_low, rhs_top, inv_low, inv_top, sizes_low, sizes_top, blocks, targets):
    rhs_low, inv_low, sizes_low = rhs_low[0, 0], inv_low[0, 0], sizes_low[0, 0]
    rhs_top, inv_top, sizes_top = rhs_top[:, 0], inv_top[:, 0], sizes_top[:, 0]
    blocks = blocks[0, :, 0, :, 0]
    targets = targets[0, :, 0, :, 0]
    per_device = sizes_low.shape[0]
    col_sups = blocks.shape[1]
    y_size = lax.axis_size("y")
    group = targets // col_sups
    turned = (group // CORES - lax.axis_index("y")) % y_size
    swapped = (group % CORES + lax.axis_index("core")) % CORES
    slots = (swapped * y_size + turned) * per_device + targets % per_device
    slots = slots.astype(jnp.int32)

    width = rhs_low.shape[-1] // CHUNKS
    top_parts = []
    pair_blocks = [stage(pair, blocks) for pair in range(blocks.shape[0])]
    cuts = [slice(chunk * width, (chunk + 1) * width) for chunk in range(CHUNKS)]
    lows = [solve(inv_low, rhs_low[:, :, cut], sizes_low) for cut in cuts]
    gathered = gather_low(*lows)
    for chunk, cut in enumerate(cuts):
        arrays, spots, order = gathered[chunk]
        use = lambda pair, seed: contribute(
            pair, pair_blocks[pair], slots, order, arrays, spots, seed
        )
        if chunk:
            arrays = lax.optimization_barrier((arrays, total))[0]
        first, total = reduce_update(use(0, None))
        second_seed = use(1, None)
        third_seed = use(2, None)
        level_one = solve(inv_top[0], rhs_top[0][:, :, cut] - first, sizes_top[0])
        arrays, spots, order = gather_shared(level_one)
        second, _ = reduce_update(use(3, second_seed))
        third_seed = use(4, third_seed)
        level_two = solve(inv_top[1], rhs_top[1][:, :, cut] - second, sizes_top[1])
        arrays, spots, order = gather_shared(level_two)
        third, _ = reduce_update(use(5, third_seed))
        level_three = solve(inv_top[2], rhs_top[2][:, :, cut] - third, sizes_top[2])
        top_parts.append(jnp.stack([level_one, level_two, level_three]))
    x_low = jnp.concatenate(lows, axis=-1)
    x_top = jnp.concatenate(top_parts, axis=-1)
    return x_low[None, None], x_top[:, None]


def solution(mesh):
    subtrees, rows, columns = (mesh.shape[name] for name in ("gz", "row", "col"))
    sizes = (subtrees, rows // X_LO, X_LO, columns // CORES, CORES)
    fine = Mesh(mesh.devices.reshape(sizes), ("gz", "z", "xl", "y", "core"))
    row, col = ("z", "xl"), ("y", "core")
    placed = (
        P("gz", col, row, None, None),
        P(None, col, row, None, None),
        P("gz", col, row, None, None),
        P(None, col, row, None, None),
        P("gz", col, row),
        P(None, col, row),
        P("gz", None, col, None, row, None, None),
        P("gz", None, col, None, row),
    )
    return jax.shard_map(
        on_device,
        mesh=fine,
        in_specs=placed,
        out_specs=(P("gz", col, row, None, None), P(None, col, row, None, None)),
        check_vma=False,
    )
```
